512 devices in a mesh: page: 16 (over z, core), row: 32 (over x, y).
Axes of the slice: x: 4, y: 8, z: 8, core: 2. Of those that a mesh axis runs over, the one named last changes fastest.
Arguments:
- qkv_rows: bfloat16 [16, 2048, 3840], P('page', 'row'), may hold values from -12 to 12
- residual: bfloat16 [16, 2048, 1280], P('page', 'row'), may hold values from -40 to 40
- out_weight: bfloat16 [1280, 1280], P('page'), may hold values from -0.15625 to 0.15625
- norm_gain: float32 [1280], replicated, may hold values from 0.1 to 1.9
- merge_weight: bfloat16 [5120, 5120], P('row'), may hold values from -0.078125 to 0.078125
- merge_bias: float32 [5120], P('row'), may hold values from -3 to 3
- page_grid: int32 [16, 2], P('page'), may hold values from 2 to 256, as said below
Outputs:
- merged: bfloat16 [16, 5120, 512], P('page', 'row')
The draws below stay inside these ranges and needn't reach their ends.
Inputs may be any that keep to these rules, and one draw needn't show every extreme that they name: `page_grid`: rows and columns are even; rows times columns is at most 2048, and one page of every draw has exactly 2048 live patches in 256 rows of 8 columns; columns are at least 8.
All inputs are finite; a program needn't handle non-finite values.
Results may differ from the reference program's by a relative error of at most 0.0049.
Values may be sent and summed in bfloat16 or wider, within the bound.
A program may use at most 64 MiB of HBM per device.

```python
import math
import jax
import jax.numpy as jnp
from jax import lax

D = 1280
HEADS = 16
MHID = 5120
HDIM = 80
PAGES = 16
PATCHES = 2048
GROUPS = 512


def draw_qkv_rows(key, part):
    keys_all = jax.random.split(key, 1)
    shape = (PAGES, PATCHES, 3 * D)
    column = jnp.arange(3 * D)[None, None, :]
    col_scale = jnp.where(column < 2 * D, 1.5, 2.0)
    base = jnp.clip(jax.random.normal(keys_all[0], shape, jnp.float32), -6.0, 6.0) * col_scale
    return base.astype(jnp.bfloat16)


def draw_residual(key, part):
    keys_all = jax.random.split(key, 3)
    shape = (PAGES, PATCHES, D)
    col_scale = jnp.exp(jax.random.uniform(keys_all[1], (1, 1, D), jnp.float32, math.log(0.3), math.log(3.0)))
    base = jnp.clip(jax.random.normal(keys_all[0], shape, jnp.float32), -6.0, 6.0)
    row_scale = jnp.exp(jax.random.uniform(keys_all[2], (PAGES, PATCHES, 1), jnp.float32, math.log(0.5), math.log(2.0)))
    base = base * col_scale * row_scale
    return base.astype(jnp.bfloat16)


def draw_page_grid(key, part):
    keys_all = jax.random.split(key, 3)
    col_cap = min(64, PATCHES // 16)
    half_cols = jax.random.randint(keys_all[0], (PAGES,), 4, col_cap + 1)
    cols_n = 2 * half_cols
    row_cap = PATCHES // (2 * cols_n)
    spread = jax.random.randint(keys_all[1], (PAGES,), 0, 1 << 20)
    half_rows = row_cap // 2 + spread % (row_cap - row_cap // 2 + 1)
    rows_n = 2 * jnp.maximum(half_rows, 1)
    forced = jax.random.randint(keys_all[2], (), 0, PAGES)
    page_ids = jnp.arange(PAGES)
    rows_n = jnp.where(page_ids == forced, PATCHES // 8, rows_n)
    cols_n = jnp.where(page_ids == forced, 8, cols_n)
    return jnp.stack([rows_n, cols_n], axis=1).astype(jnp.int32)


def block_levels(stream_key, shape, cuts, least, top_value):
    level = 1.0
    for position, shards_of in cuts:
        heights = jax.random.uniform(jax.random.fold_in(jax.random.fold_in(stream_key, 6), position), (shards_of,), jnp.float32, least / len(cuts), top_value / len(cuts))
        level = level * jnp.repeat(jnp.exp(heights), shape[position] // shards_of).reshape((-1,) + (1,) * (len(shape) - 1 - position))
    return level


def centred(rng, dims, scale, limit, cuts=(), kind=jnp.bfloat16):
    gain = block_levels(rng, dims, cuts, -0.22, 0.18) if cuts else 1.0
    entries = jax.random.normal(rng, dims, jnp.float32) * scale * gain
    return jnp.minimum(jnp.maximum(entries, -limit), limit).astype(kind)


def setup_inputs(seed: int = 0) -> dict:
    key_list = jax.random.split(jax.random.key(seed), 8)
    return {
        "qkv_rows": draw_qkv_rows(jax.random.fold_in(key_list[7], 71), 0),
        "residual": draw_residual(jax.random.fold_in(key_list[7], 71), 0),
        "out_weight": centred(key_list[2], (D, D), D ** -0.5, 0.15625, ((0, 16),)),
        "norm_gain": jnp.clip(1.0 + 0.18 * jax.random.normal(key_list[3], (D,), jnp.float32), 0.1, 1.9),
        "merge_weight": centred(key_list[4], (MHID, 4 * D), (4 * D) ** -0.5, 0.078125, ((0, 32),)),
        "merge_bias": centred(key_list[5], (MHID,), 0.5, 3.0, ((0, 32),), jnp.float32),
        "page_grid": draw_page_grid(jax.random.fold_in(key_list[7], 71), 0),
    }


def head_attention(operands, key_valid):
    queries, key_rows, value_rows = operands
    scores = jnp.dot(queries, key_rows.T, preferred_element_type=jnp.float32) / math.sqrt(HDIM)
    scores = jnp.where(key_valid[None, :], scores, -1e+30)
    peak = lax.optimization_barrier(jnp.max(scores, axis=1, keepdims=True))
    weights = jnp.exp(scores - peak)
    total = lax.optimization_barrier(jnp.sum(weights, axis=1, keepdims=True))
    probs = weights.astype(jnp.bfloat16)
    mixed = jnp.dot(probs, value_rows, preferred_element_type=jnp.float32) / total
    return mixed.astype(jnp.bfloat16)

def group_index(grid_row):
    rows_n = grid_row[0]
    cols_n = grid_row[1]
    slots = jnp.arange(GROUPS, dtype=jnp.int32)
    half_cols = cols_n // 2
    live = slots < rows_n // 2 * half_cols
    first = jnp.where(live, 2 * (slots // half_cols) * cols_n + 2 * (slots % half_cols), 0).astype(jnp.int32)
    return (live, [first, first + 1, first + cols_n, first + cols_n + 1])

def reference(qkv_rows, residual, out_weight, norm_gain, merge_weight, merge_bias, page_grid):

    def page_layer(operands):
        page_qkv, page_resid, grid_row = operands
        valid_len = grid_row[0] * grid_row[1]
        key_valid = jnp.arange(PATCHES, dtype=jnp.int32) < valid_len
        queries = page_qkv[:, :D].reshape(PATCHES, HEADS, HDIM).transpose(1, 0, 2)
        key_rows = page_qkv[:, D:2 * D].reshape(PATCHES, HEADS, HDIM).transpose(1, 0, 2)
        value_rows = page_qkv[:, 2 * D:].reshape(PATCHES, HEADS, HDIM).transpose(1, 0, 2)
        heads_out = lax.map(lambda ops: head_attention(ops, key_valid), (queries, key_rows, value_rows))
        attn = heads_out.transpose(1, 0, 2).reshape(PATCHES, D)
        hidden = page_resid.astype(jnp.float32) + jnp.dot(attn, out_weight, preferred_element_type=jnp.float32)
        normed = (hidden * lax.rsqrt(lax.optimization_barrier(jnp.mean(hidden * hidden, axis=1, keepdims=True)) + 1e-06) * norm_gain).astype(jnp.bfloat16)
        live, corners = group_index(grid_row)
        grouped = jnp.concatenate([jnp.take(normed, corner, axis=0) for corner in corners], axis=1)
        merged = jnp.dot(merge_weight, grouped.T, preferred_element_type=jnp.float32) + merge_bias[:, None]
        merged = jax.nn.gelu(merged, approximate=False)
        return jnp.where(live[None, :], merged, 0.0).astype(jnp.bfloat16)
    return lax.map(page_layer, (qkv_rows, residual, page_grid))
```

```python
import functools
import math

import jax
import jax.numpy as jnp
from jax import lax
from jax.experimental import pallas as pl
from jax.experimental.pallas import tpu as pltpu
from jax.sharding import PartitionSpec as P

D = 1280
HEADS = 16
HDIM = 80
MESH = pl.DeviceIdType.MESH
F32 = jnp.float32
BF16 = jnp.bfloat16
BIG = -1e30


def rcopy(src, dst, send_sem, recv_sem, dev):
    return pltpu.make_async_remote_copy(
        src_ref=src, dst_ref=dst, send_sem=send_sem, recv_sem=recv_sem,
        device_id=dev, device_id_type=MESH,
    )


def nt(a, b):
    return lax.dot_general(a, b, (((1,), (1,)), ((), ())), preferred_element_type=F32)


def kernel(
    grid_ref, qkv_ref, res_ref, wo_ref, gain_ref, bias_ref, w_ref,
    out_ref,
    pack_buf, xbuf, obuf, abuf, wo_pad, wsl, nsend, nall, own_part, part_send, part_recv,
    p1_send, p1_recv, fw_send, fw_recv, ret_send, ret_recv,
    w_send, w_recv, wf_send, wf_recv,
    z_send, z_recv, zf_send, zf_recv,
    xa_send, xa_recv, y_send, y_recv, rs_send, rs_recv, loc_sem,
):
    page = lax.axis_index("page")
    row = lax.axis_index("row")
    core = page % 2
    zi = page // 2
    par = row % 2
    me16 = row // 2
    xi = row // 8
    yi = row % 8
    peer_page = page - core + par
    sib = (page - core + 1 - core, row)
    is_self = par == core
    y_right = (page, xi * 8 + (yi + 1) % 8)
    y_left = (page, xi * 8 + (yi + 7) % 8)
    z_right = (((zi + 1) % 8) * 2 + core, row)
    z_left = (((zi + 7) % 8) * 2 + core, row)

    def xdev(j):
        return (page, ((xi + j) % 4) * 8 + yi)

    def peer(s):
        return (peer_page, 2 * s + core)

    barrier = pltpu.get_barrier_semaphore()

    def greet(dev):
        pl.semaphore_signal(barrier, inc=1, device_id=dev, device_id_type=MESH)

    for dev in (sib, y_right, y_left, z_right, z_left):
        greet(dev)

    def greet_peer(i, carry):
        greet(peer((me16 + i) % 16))
        return carry

    lax.fori_loop(1, 16, greet_peer, 0)

    @pl.when(jnp.logical_not(is_self))
    def _():
        greet(peer(me16))
        for j in (1, 2, 3):
            greet(xdev(j))

    rows_n = grid_ref[0, 0]
    cols_n = grid_ref[0, 1]
    valid_len = rows_n * cols_n
    lane = lax.broadcasted_iota(jnp.int32, (64, 256), 1)
    slot = row * 64 + lax.broadcasted_iota(jnp.int32, (64, 256), 0)
    tail = jnp.where(
        lane == 240, jnp.where(slot < valid_len, 0.0, BIG), jnp.where(lane == 241, 1.0, 0.0)
    )
    for h in range(HEADS):
        val = tail
        for third in (2, 1, 0):
            start = third * D + h * HDIM
            base = min(start // 128 * 128, 3 * D - 256)
            dest = third * HDIM
            window = qkv_ref[0, :, base : base + 256].astype(F32)
            shift = (dest - (start - base)) % 256
            if shift:
                window = pltpu.roll(window, shift, axis=1)
            val = jnp.where((lane >= dest) & (lane < dest + HDIM), window, val)
        pack_buf[h] = val.astype(BF16)

    @pl.when(is_self)
    def _():
        pl.semaphore_wait(barrier, 20)

    @pl.when(jnp.logical_not(is_self))
    def _():
        pl.semaphore_wait(barrier, 24)

    def z_slot(ref, dist, direction, half):
        src_z = (zi - dist + 8) % 8 if direction == 0 else (zi + dist) % 8
        return ref.at[src_z * 2 + core, 32:112, half * 640 : half * 640 + 640]

    def z_limit(direction, half):
        return 4 if direction == half else 3

    def z_copy(dist, direction, half):
        if dist == 1:
            src = wo_ref.at[:, half * 640 : half * 640 + 640]
        else:
            src = z_slot(wo_pad, dist - 1, direction, half)
        return rcopy(
            src, z_slot(wo_pad, dist - 1, direction, half),
            z_send.at[direction, half, dist - 1], z_recv.at[direction, half, dist - 1],
            z_right if direction == 0 else z_left,
        )

    def z_fwd(dist, direction, half):
        place = z_slot(wo_pad, dist, direction, half)
        return rcopy(
            place, place, zf_send.at[direction, half, dist - 1],
            zf_recv.at[direction, half, dist - 1], sib,
        )

    for direction in (0, 1):
        for half in (0, 1):
            z_copy(1, direction, half).start()

    def p1_copy(i):
        h = (me16 + i) % 16
        return rcopy(
            pack_buf.at[h], xbuf.at[0, me16], p1_send.at[h], p1_recv.at[me16], peer(h)
        )

    p1_local = pltpu.make_async_copy(pack_buf.at[me16], xbuf.at[0, me16], p1_recv.at[me16])

    @pl.when(is_self)
    def _():
        p1_local.start()

    @pl.when(jnp.logical_not(is_self))
    def _():
        p1_copy(0).start()

    def p1_start(i, carry):
        p1_copy(i).start()
        return carry

    lax.fori_loop(1, 16, p1_start, 0)

    own_wo = pltpu.make_async_copy(wo_ref, wo_pad.at[page, 32:112, :], loc_sem.at[0])
    own_wo.start()
    sib_wo = rcopy(wo_ref, wo_pad.at[page, 32:112, :], loc_sem.at[1], loc_sem.at[2], sib)
    sib_wo.start()
    for h in range(HEADS):
        wo_pad[h, 0:32, :] = jnp.zeros((32, D), BF16)
        wo_pad[h, 112:128, :] = jnp.zeros((16, D), BF16)

    def fw_copy(s):
        return rcopy(xbuf.at[0, s], xbuf.at[1, s], fw_send.at[s], fw_recv.at[s], sib)

    def p1_take(i, carry):
        s = (me16 + 16 - i) % 16
        rcopy(xbuf.at[0, s], xbuf.at[0, s], p1_send.at[s], p1_recv.at[s], sib).wait_recv()
        fw_copy(s).start()
        return carry

    @pl.when(is_self)
    def _():
        p1_local.wait()
        fw_copy(me16).start()

    @pl.when(jnp.logical_not(is_self))
    def _():
        p1_take(0, 0)

    for dist in (1, 2, 3, 4):
        lax.fori_loop(4 * dist - 3, min(16, 4 * dist + 1), p1_take, 0)
        for direction in (0, 1):
            for half in (0, 1):
                if dist > z_limit(direction, half):
                    continue
                place = z_slot(wo_pad, dist, direction, half)
                rcopy(
                    place, place, z_send.at[direction, half, dist - 1],
                    z_recv.at[direction, half, dist - 1], sib,
                ).wait_recv()
                if dist < z_limit(direction, half):
                    z_copy(dist + 1, direction, half).start()
                z_fwd(dist, direction, half).start()

    def w_copy(j, di):
        xd = (xi + j) % 4
        col = pl.multiple_of((2 * di + xd // 2) * D + (xd % 2) * 640, 128)
        lines = pl.ds(pl.multiple_of(core * 80, 16), 80)
        return rcopy(
            w_ref.at[lines, pl.ds(col, 640)], wsl.at[xi, di, lines, :],
            w_send.at[j - 1, di], w_recv.at[j - 1, di], xdev(j),
        )

    def w_fwd(j, di):
        xs = (xi + 4 - j) % 4
        lines = pl.ds(pl.multiple_of(core * 80, 16), 80)
        place = wsl.at[xs, di, lines, :]
        return rcopy(place, place, wf_send.at[j - 1, di], wf_recv.at[j - 1, di], sib)

    for j in (1, 3, 2):
        for di in (0, 1):
            w_copy(j, di).start()
    w_local = []
    for di in (0, 1):
        col = pl.multiple_of((2 * di + xi // 2) * D + (xi % 2) * 640, 128)
        w_local.append(
            pltpu.make_async_copy(w_ref.at[:, pl.ds(col, 640)], wsl.at[xi, di], loc_sem.at[4 + di])
        )
        w_local[di].start()

    def fw_take(s, carry):
        rcopy(xbuf.at[1, s], xbuf.at[1, s], fw_send.at[s], fw_recv.at[s], sib).wait_recv()
        return carry

    lax.fori_loop(0, 16, fw_take, 0)
    factor = math.log2(math.e) / math.sqrt(HDIM)
    lane_q = lax.broadcasted_iota(jnp.int32, (256, 256), 1)

    def ret_copy(s):
        return rcopy(obuf.at[s], abuf.at[me16], ret_send.at[s], ret_recv.at[me16], peer(s))

    ret_local = pltpu.make_async_copy(obuf.at[me16], abuf.at[me16], ret_recv.at[me16])

    def attend(i, carry):
        blk = (i + me16) % 4
        queries = xbuf[0, pl.ds(4 * blk, 4)].reshape(256, 256).astype(F32)
        rolled = pltpu.roll(queries, HDIM, axis=1)
        rolled = jnp.where(
            (lane_q >= HDIM) & (lane_q < 2 * HDIM), rolled, jnp.where(lane_q == 240, 1.0, 0.0)
        ).astype(BF16)
        keys = xbuf[...].reshape(2048, 256)
        scores = nt(rolled, keys)
        peak = jnp.max(scores, axis=1, keepdims=True)
        weights = jnp.exp2((scores - peak) * factor).astype(BF16)
        mixed = jnp.dot(weights, keys, preferred_element_type=F32)[:, 128:]
        mixed = mixed / mixed[:, 113:114]
        obuf[pl.ds(4 * blk, 4)] = mixed.astype(BF16).reshape(4, 64, 128)
        for j in range(4):
            s = 4 * blk + (j + row // 8) % 4
            own = jnp.logical_and(is_self, s == me16)

            @pl.when(own)
            def _():
                ret_local.start()

            @pl.when(jnp.logical_not(own))
            def _():
                ret_copy(s).start()

        return carry

    lax.fori_loop(0, 4, attend, 0)

    own_wo.wait()
    sib_page = page - core + 1 - core
    rcopy(wo_ref, wo_pad.at[sib_page, 32:112, :], loc_sem.at[1], loc_sem.at[2], sib).wait_recv()
    for dist in (1, 2, 3, 4):
        for direction in (0, 1):
            for half in (0, 1):
                if dist > z_limit(direction, half):
                    continue
                src_z = (zi - dist + 8) % 8 if direction == 0 else (zi + dist) % 8
                place = wo_pad.at[src_z * 2 + 1 - core, 32:112, half * 640 : half * 640 + 640]
                rcopy(
                    place, place, zf_send.at[direction, half, dist - 1],
                    zf_recv.at[direction, half, dist - 1], sib,
                ).wait_recv()

    def ret_take(h, carry):
        own = jnp.logical_and(is_self, h == me16)

        @pl.when(own)
        def _():
            ret_local.wait()

        @pl.when(jnp.logical_not(own))
        def _():
            rcopy(abuf.at[h], abuf.at[h], ret_send.at[h], ret_recv.at[h], sib).wait_recv()

        return carry

    lax.fori_loop(0, 16, ret_take, 0)
    attn = jnp.concatenate([abuf[h] for h in range(HEADS)], axis=1)
    hidden = res_ref[0].astype(F32) + jnp.dot(
        attn, wo_pad[...].reshape(HEADS * 128, D), preferred_element_type=F32
    )
    mean_sq = jnp.mean(hidden * hidden, axis=1, keepdims=True)
    normed = (hidden * lax.rsqrt(mean_sq + 1e-06) * gain_ref[...]).astype(BF16)
    dst_r = lax.broadcasted_iota(jnp.int32, (64, 64), 0)
    src_r = lax.broadcasted_iota(jnp.int32, (64, 64), 1)
    want = jnp.where(dst_r < 32, 2 * dst_r, 2 * dst_r - 63)
    select = jnp.where(src_r == want, 1.0, 0.0).astype(BF16)
    split = jnp.dot(select, normed, preferred_element_type=F32).astype(BF16)
    for xd in range(4):
        dj, fh = xd // 2, xd % 2
        nsend[xd] = split[32 * dj : 32 * dj + 32, 640 * fh : 640 * fh + 640]

    def xa_copy(j):
        return rcopy(
            nsend.at[(xi + j) % 4], nall.at[xi, yi], xa_send.at[j - 1], xa_recv.at[j - 1], xdev(j)
        )

    for j in (1, 3, 2):
        xa_copy(j).start()
    xa_local = pltpu.make_async_copy(nsend.at[xi], nall.at[xi, yi], loc_sem.at[3])
    xa_local.start()

    def y_slot(j, dist, direction):
        xs = (xi + 4 - j) % 4
        ys = (yi - dist + 8) % 8 if direction == 0 else (yi + dist) % 8
        return nall.at[xs, ys]

    def y_limit(j, direction):
        return 4 if direction == j // 2 else 3

    def y_copy(j, dist, direction):
        place = y_slot(j, dist - 1, direction)
        return rcopy(
            place, place, y_send.at[j, direction, dist - 1], y_recv.at[j, direction, dist - 1],
            y_right if direction == 0 else y_left,
        )

    def y_wait(j, dist, direction):
        place = y_slot(j, dist, direction)
        rcopy(
            place, place, y_send.at[j, direction, dist - 1], y_recv.at[j, direction, dist - 1], sib
        ).wait_recv()

    xa_local.wait()
    for j in (0, 1, 3, 2):
        if j:
            xs = (xi + 4 - j) % 4
            rcopy(
                nall.at[xs, yi], nall.at[xs, yi], xa_send.at[j - 1], xa_recv.at[j - 1], sib
            ).wait_recv()
        for direction in (0, 1):
            y_copy(j, 1, direction).start()
    for dist in (1, 2, 3, 4):
        for j in (0, 1, 3, 2):
            for direction in (0, 1):
                if dist > y_limit(j, direction):
                    continue
                y_wait(j, dist, direction)
                if dist < y_limit(j, direction):
                    y_copy(j, dist + 1, direction).start()
        if dist == 1:
            for j in (1, 3, 2):
                for di in (0, 1):
                    xs = (xi + 4 - j) % 4
                    lines = pl.ds(pl.multiple_of(core * 80, 16), 80)
                    place = wsl.at[xs, di, lines, :]
                    rcopy(
                        place, place, w_send.at[j - 1, di], w_recv.at[j - 1, di], sib
                    ).wait_recv()
                    w_fwd(j, di).start()
    for j in (1, 3, 2):
        for di in (0, 1):
            xs = (xi + 4 - j) % 4
            lines = pl.ds(pl.multiple_of((1 - core) * 80, 16), 80)
            place = wsl.at[xs, di, lines, :]
            rcopy(place, place, wf_send.at[j - 1, di], wf_recv.at[j - 1, di], sib).wait_recv()
    for di in (0, 1):
        w_local[di].wait()

    half_c = cols_n // 2
    half_f = half_c.astype(F32)

    def rs_copy(b, j):
        return rcopy(
            part_send.at[b, (xi + j) % 4], part_recv.at[b, j - 1],
            rs_send.at[b, j - 1], rs_recv.at[b, j - 1], xdev(j),
        )

    for b in (0, 1):
        first = 384 * b
        group = (256 * b + lax.broadcasted_iota(jnp.int32, (256, 640), 0)).astype(F32)
        place = (first + lax.broadcasted_iota(jnp.int32, (256, 640), 1)).astype(F32)
        band = jnp.floor((group + 0.5) / half_f)
        total = None
        window = nall[...].reshape(1024, 640)[first : first + 640]
        for di in (0, 1):
            want = band * half_f + group + di * half_f
            pick = jnp.where(place == want, 1.0, 0.0).astype(BF16)
            rows_g = jnp.dot(pick, window, preferred_element_type=F32).astype(BF16)
            term = nt(wsl[:, di].reshape(640, 640), rows_g)
            total = term if total is None else total + term
        pieces = total.reshape(4, 160, 256)
        own_part[b] = pieces
        part_send[b] = pieces.astype(BF16)
        for j in (1, 3, 2):
            rs_copy(b, j).start()

    eye = lax.broadcasted_iota(jnp.int32, (160, 160), 0) == lax.broadcasted_iota(
        jnp.int32, (160, 160), 1
    )
    bias = jnp.sum(jnp.where(eye, bias_ref[...], 0.0), axis=1, keepdims=True)
    live_groups = (rows_n // 2) * half_c
    for b in (0, 1):
        total = own_part[b, xi] + bias
        for j in (1, 3, 2):
            rcopy(
                part_send.at[b, 0], part_recv.at[b, j - 1],
                rs_send.at[b, j - 1], rs_recv.at[b, j - 1], sib,
            ).wait_recv()
            total = total + part_recv[b, j - 1].astype(F32)
        act = 0.5 * total * (1.0 + lax.erf(total * math.sqrt(0.5)))
        group = 256 * b + lax.broadcasted_iota(jnp.int32, (160, 256), 1)
        act = jnp.where(group < live_groups, act, 0.0)
        out_ref[0, :, 256 * b : 256 * b + 256] = act.astype(BF16)

    @pl.when(jnp.logical_not(is_self))
    def _():
        p1_copy(0).wait_send()

    def p1_sent(i, carry):
        p1_copy(i).wait_send()
        return carry

    lax.fori_loop(1, 16, p1_sent, 0)

    def sent(s, carry):
        fw_copy(s).wait_send()
        own = jnp.logical_and(is_self, s == me16)

        @pl.when(jnp.logical_not(own))
        def _():
            ret_copy(s).wait_send()

        return carry

    lax.fori_loop(0, 16, sent, 0)
    sib_wo.wait_send()
    for dist in (1, 2, 3, 4):
        for direction in (0, 1):
            for half in (0, 1):
                if dist <= z_limit(direction, half):
                    z_copy(dist, direction, half).wait_send()
                    z_fwd(dist, direction, half).wait_send()
            for j in range(4):
                if dist <= y_limit(j, direction):
                    y_copy(j, dist, direction).wait_send()
    for j in (1, 2, 3):
        xa_copy(j).wait_send()
        for di in (0, 1):
            w_copy(j, di).wait_send()
            w_fwd(j, di).wait_send()
            rs_copy(di, j).wait_send()


def local(qkv_rows, residual, out_weight, norm_gain, merge_weight, merge_bias, page_grid):
    vmem = pl.BlockSpec(memory_space=pltpu.VMEM)
    dma = pltpu.SemaphoreType.DMA
    return pl.pallas_call(
        kernel,
        out_shape=jax.ShapeDtypeStruct((1, 160, 512), BF16),
        in_specs=[pl.BlockSpec(memory_space=pltpu.SMEM)] + [vmem] * 5
        + [pl.BlockSpec(memory_space=pl.ANY)],
        out_specs=vmem,
        scratch_shapes=[
            pltpu.VMEM((16, 64, 256), BF16),
            pltpu.VMEM((2, 16, 64, 256), BF16),
            pltpu.VMEM((16, 64, 128), BF16),
            pltpu.VMEM((16, 64, 128), BF16),
            pltpu.VMEM((16, 128, D), BF16),
            pltpu.VMEM((4, 2, 160, 640), BF16),
            pltpu.VMEM((4, 32, 640), BF16),
            pltpu.VMEM((4, 8, 32, 640), BF16),
            pltpu.VMEM((2, 4, 160, 256), F32),
            pltpu.VMEM((2, 4, 160, 256), BF16),
            pltpu.VMEM((2, 3, 160, 256), BF16),
            dma((16,)), dma((16,)), dma((16,)), dma((16,)), dma((16,)), dma((16,)),
            dma((3, 2)), dma((3, 2)), dma((3, 2)), dma((3, 2)),
            dma((2, 2, 4)), dma((2, 2, 4)), dma((2, 2, 4)), dma((2, 2, 4)),
            dma((3,)), dma((3,)), dma((4, 2, 4)), dma((4, 2, 4)), dma((2, 3)), dma((2, 3)),
            dma((6,)),
        ],
        compiler_params=pltpu.CompilerParams(
            collective_id=0, has_side_effects=True, vmem_limit_bytes=48 * 1024 * 1024
        ),
        cost_estimate=pl.CostEstimate(
            flops=4 * 10**9, bytes_accessed=4 * 10**6, transcendentals=2 * 10**6
        ),
        name="sublayer",
    )(
        page_grid, qkv_rows, residual, out_weight, norm_gain.reshape(1, D),
        merge_bias.reshape(1, 160), merge_weight,
    )


def solution(mesh):
    in_specs = (
        P("page", "row", None),
        P("page", "row", None),
        P("page", None),
        P(),
        P("row", None),
        P("row"),
        P("page", None),
    )
    out_specs = P("page", "row", None)
    return jax.shard_map(local, mesh=mesh, in_specs=in_specs, out_specs=out_specs, check_vma=False)
```

```python
import functools
import math

import jax
import jax.numpy as jnp
from jax import lax
from jax.experimental import pallas as pl
from jax.experimental.pallas import tpu as pltpu
from jax.sharding import PartitionSpec as P

D = 1280
HEADS = 16
HDIM = 80
MESH = pl.DeviceIdType.MESH
F32 = jnp.float32
BF16 = jnp.bfloat16
BIG = -1e30
ZORDER = (1, 7, 2, 6, 3, 5, 4)
ORDER = tuple((n // 4, n % 4) for n in range(1, 16)) + ((0, 0),)


def rcopy(src, dst, send_sem, recv_sem, dev):
    return pltpu.make_async_remote_copy(
        src_ref=src, dst_ref=dst, send_sem=send_sem, recv_sem=recv_sem,
        device_id=dev, device_id_type=MESH,
    )


def nt(a, b):
    return lax.dot_general(a, b, (((1,), (1,)), ((), ())), preferred_element_type=F32)


def kernel(
    grid_hbm, qkv_hbm, res_hbm, wo_ref, gain_hbm, bias_hbm, w_ref,
    out_ref,
    grid_ref, qkv_ref, res_ref, gain_ref, bias_ref,
    pack_buf, xbuf, qbuf, sbuf, obuf, abuf, wo_pad, wsl, nsend, nall, own_part, part_send, part_recv,
    p1_send, p1_recv, fw_send, fw_recv, ret_send, ret_recv,
    w_send, w_recv, wf_send, wf_recv,
    z_send, z_recv, zx_send, zx_recv, zf_send, zf_recv,
    xa_send, xa_recv, y_send, y_recv, rs_send, rs_recv, loc_sem,
):
    page = lax.axis_index("page")
    row = lax.axis_index("row")
    core = page % 2
    zi = page // 2
    par = row % 2
    me16 = row // 2
    xi = row // 8
    yi = row % 8
    peer_page = page - core + par
    sib = (page - core + 1 - core, row)
    is_self = par == core
    y_right = (page, xi * 8 + (yi + 1) % 8)
    y_left = (page, xi * 8 + (yi + 7) % 8)

    def zdev(dz):
        return ((zi + dz) % 8 * 2 + core, row)

    def xdev(j):
        return (page, ((xi + j) % 4) * 8 + yi)

    def peer(s):
        return (peer_page, 2 * s + core)

    pulls = [
        pltpu.make_async_copy(src, dst, loc_sem.at[7 + n])
        for n, (src, dst) in enumerate(
            (
                (grid_hbm, grid_ref), (qkv_hbm, qkv_ref), (res_hbm, res_ref),
                (gain_hbm, gain_ref), (bias_hbm, bias_ref),
            )
        )
    ]
    for pull in pulls:
        pull.start()

    own_wo = pltpu.make_async_copy(wo_ref, wo_pad.at[page, 32:112, :], loc_sem.at[0])
    own_wo.start()

    barrier = pltpu.get_barrier_semaphore()

    def greet(dev):
        pl.semaphore_signal(barrier, inc=1, device_id=dev, device_id_type=MESH)

    def next_y(j, direction):
        return (page, (xi + j) % 4 * 8 + (yi + 1 + 6 * direction) % 8)

    greet(sib)
    for dz in ZORDER:
        greet(zdev(dz))
    for j in range(4):
        greet(next_y(j, 0))
        greet(next_y(j, 1))

    def greet_peer(i, carry):
        greet(peer((me16 + i) % 16))
        return carry

    lax.fori_loop(1, 16, greet_peer, 0)

    @pl.when(jnp.logical_not(is_self))
    def _():
        greet(peer(me16))
        for j in (1, 2, 3):
            greet(xdev(j))

    pulls[0].wait()
    rows_n = grid_ref[0, 0]
    cols_n = grid_ref[0, 1]
    valid_len = rows_n * cols_n
    lane = lax.broadcasted_iota(jnp.int32, (64, 256), 1)
    slot = row * 64 + lax.broadcasted_iota(jnp.int32, (64, 256), 0)
    tail = jnp.where(
        lane == 240, jnp.where(slot < valid_len, 0.0, BIG), jnp.where(lane == 241, 1.0, 0.0)
    )

    def pack(h):
        val = tail
        for third in (2, 1, 0):
            start = third * D + h * HDIM
            base = pl.multiple_of(jnp.minimum(start // 128 * 128, 3 * D - 256), 128)
            dest = third * HDIM
            window = qkv_ref[0, :, pl.ds(base, 256)].astype(F32)
            window = pltpu.roll(window, (dest + 256 - (start - base)) % 256, axis=1)
            val = jnp.where((lane >= dest) & (lane < dest + HDIM), window, val)
        pack_buf[h] = val.astype(BF16)

    @pl.when(is_self)
    def _():
        pl.semaphore_wait(barrier, 31)

    @pl.when(jnp.logical_not(is_self))
    def _():
        pl.semaphore_wait(barrier, 35)

    my_col = pl.multiple_of(xi % 2 * 640, 128)
    other_col = pl.multiple_of(640 - xi % 2 * 640, 128)
    x_side = (page, (xi + 5 - 2 * core) % 4 * 8 + yi)

    def z_page(dz, of_core):
        return (zi + 8 - dz) % 8 * 2 + of_core

    def z_copy(dz):
        return rcopy(
            wo_pad.at[page, 32:112, pl.ds(my_col, 640)], wo_pad.at[page, 32:112, pl.ds(my_col, 640)],
            z_send.at[dz - 1], z_recv.at[dz - 1], zdev(dz),
        )

    def zx_copy(dz):
        place = wo_pad.at[z_page(dz, core), 32:112, pl.ds(my_col, 640)]
        return rcopy(place, place, zx_send.at[dz - 1], zx_recv.at[dz - 1], x_side)

    def zf_copy(dz, of_core):
        place = wo_pad.at[z_page(dz, of_core), 32:112, :]
        return rcopy(place, place, zf_send.at[dz - 1], zf_recv.at[dz - 1], sib)

    def z_step(dz):
        place = wo_pad.at[z_page(dz, core), 32:112, pl.ds(my_col, 640)]
        rcopy(place, place, z_send.at[dz - 1], z_recv.at[dz - 1], sib).wait_recv()
        zx_copy(dz).start()

    def zx_step(dz):
        place = wo_pad.at[z_page(dz, core), 32:112, pl.ds(other_col, 640)]
        rcopy(place, place, zx_send.at[dz - 1], zx_recv.at[dz - 1], sib).wait_recv()
        zf_copy(dz, core).start()

    half_y = yi // 2

    def p1_copy(n):
        dx, dy = ORDER[n]
        h = (xi + dx) % 4 * 4 + (half_y + dy) % 4
        return rcopy(
            pack_buf.at[h], xbuf.at[0, me16], p1_send.at[h], p1_recv.at[me16], peer(h)
        )

    p1_local = pltpu.make_async_copy(pack_buf.at[me16], xbuf.at[0, me16], p1_recv.at[me16])

    pulls[1].wait()
    for n in range(15):
        dx, dy = ORDER[n]
        pack((xi + dx) % 4 * 4 + (half_y + dy) % 4)
        p1_copy(n).start()
    pack(me16)

    @pl.when(is_self)
    def _():
        p1_local.start()

    @pl.when(jnp.logical_not(is_self))
    def _():
        p1_copy(15).start()

    own_wo.wait()
    for dz in ZORDER:
        z_copy(dz).start()

    def w_copy(j, di):
        xd = (xi + j) % 4
        col = pl.multiple_of((2 * di + xd // 2) * D + (xd % 2) * 640, 128)
        lines = pl.ds(pl.multiple_of(core * 80, 16), 80)
        return rcopy(
            w_ref.at[lines, pl.ds(col, 640)], wsl.at[xi, di, lines, :],
            w_send.at[j - 1, di], w_recv.at[j - 1, di], xdev(j),
        )

    def w_fwd(j, di):
        xs = (xi + 4 - j) % 4
        lines = pl.ds(pl.multiple_of(core * 80, 16), 80)
        place = wsl.at[xs, di, lines, :]
        return rcopy(place, place, wf_send.at[j - 1, di], wf_recv.at[j - 1, di], sib)

    for j in (1, 3, 2):
        for di in (0, 1):
            w_copy(j, di).start()
    w_local = []
    for di in (0, 1):
        col = pl.multiple_of((2 * di + xi // 2) * D + (xi % 2) * 640, 128)
        w_local.append(
            pltpu.make_async_copy(w_ref.at[:, pl.ds(col, 640)], wsl.at[xi, di], loc_sem.at[4 + di])
        )
        w_local[di].start()
    sib_wo = rcopy(wo_pad.at[page, 32:112, :], wo_pad.at[page, 32:112, :], loc_sem.at[1], loc_sem.at[2], sib)
    sib_wo.start()
    for h in range(HEADS):
        wo_pad[h, 0:32, :] = jnp.zeros((32, D), BF16)
        wo_pad[h, 112:128, :] = jnp.zeros((16, D), BF16)

    def fw_copy(s):
        return rcopy(xbuf.at[0, s], xbuf.at[1, s], fw_send.at[s], fw_recv.at[s], sib)

    def p1_take(n):
        dx, dy = ORDER[n]
        s = (xi + 4 - dx) % 4 * 4 + (half_y + 4 - dy) % 4
        rcopy(xbuf.at[0, s], xbuf.at[0, s], p1_send.at[s], p1_recv.at[s], sib).wait_recv()
        fw_copy(s).start()

    @pl.when(is_self)
    def _():
        p1_local.wait()
        fw_copy(me16).start()

    for n in range(15):
        p1_take(n)

    @pl.when(jnp.logical_not(is_self))
    def _():
        p1_take(15)

    for dz in ZORDER:
        z_step(dz)

    factor = math.log2(math.e) / math.sqrt(HDIM)
    lane_q = lax.broadcasted_iota(jnp.int32, (256, 256), 1)

    def owner(n):
        dx, dy = ORDER[n]
        return (xi + dx) % 4 * 4 + (half_y + dy) % 4

    def ret_copy(half, n):
        return rcopy(
            obuf.at[half, n], abuf.at[half, me16],
            ret_send.at[half, n], ret_recv.at[half, me16], peer(owner(n)),
        )

    def ret_local(half):
        return pltpu.make_async_copy(
            obuf.at[half, 15], abuf.at[half, me16], ret_recv.at[half, me16]
        )

    def rolled_queries(blk):
        half, first = blk // 2, blk % 2 * 8
        queries = jnp.concatenate(
            [xbuf[0, owner(n), 32 * half : 32 * half + 32] for n in range(first, first + 8)], axis=0
        )
        rolled = pltpu.roll(queries.astype(F32), HDIM, axis=1)
        return jnp.where(
            (lane_q >= HDIM) & (lane_q < 2 * HDIM), rolled, jnp.where(lane_q == 240, 1.0, 0.0)
        ).astype(BF16)

    for blk in range(4):
        qbuf[blk] = rolled_queries(blk)
        sbuf[blk] = nt(qbuf[blk], xbuf[0].reshape(1024, 256))

    def fw_take(s, carry):
        rcopy(xbuf.at[1, s], xbuf.at[1, s], fw_send.at[s], fw_recv.at[s], sib).wait_recv()
        return carry

    lax.fori_loop(0, 16, fw_take, 0)
    later = nt(qbuf[0], xbuf[1].reshape(1024, 256))
    for blk in range(4):
        there = later
        if blk < 3:
            later = nt(qbuf[blk + 1], xbuf[1].reshape(1024, 256))
        here = sbuf[blk]
        peak = jnp.maximum(
            jnp.max(here, axis=1, keepdims=True), jnp.max(there, axis=1, keepdims=True)
        )
        mixed = jnp.dot(
            jnp.exp2((here - peak) * factor).astype(BF16), xbuf[0].reshape(1024, 256),
            preferred_element_type=F32,
        ) + jnp.dot(
            jnp.exp2((there - peak) * factor).astype(BF16), xbuf[1].reshape(1024, 256),
            preferred_element_type=F32,
        )
        mixed = mixed[:, 128:]
        mixed = mixed / mixed[:, 113:114]
        half, first = blk // 2, blk % 2 * 8
        obuf[half, first : first + 8] = mixed.astype(BF16).reshape(8, 32, 128)
        for n in range(first, min(first + 8, 15)):
            ret_copy(half, n).start()

    @pl.when(is_self)
    def _():
        ret_local(0).start()
        ret_local(1).start()

    @pl.when(jnp.logical_not(is_self))
    def _():
        ret_copy(0, 15).start()
        ret_copy(1, 15).start()

    for dz in ZORDER:
        zx_step(dz)

    for j in (1, 3, 2):
        for di in (0, 1):
            xs = (xi + 4 - j) % 4
            lines = pl.ds(pl.multiple_of(core * 80, 16), 80)
            place = wsl.at[xs, di, lines, :]
            rcopy(place, place, w_send.at[j - 1, di], w_recv.at[j - 1, di], sib).wait_recv()
            w_fwd(j, di).start()

    sib_page = page - core + 1 - core
    rcopy(wo_ref, wo_pad.at[sib_page, 32:112, :], loc_sem.at[1], loc_sem.at[2], sib).wait_recv()
    for dz in ZORDER:
        zf_copy(dz, 1 - core).wait_recv()
    pulls[2].wait()
    pulls[3].wait()
    dst_r = lax.broadcasted_iota(jnp.int32, (32, 32), 0)
    src_r = lax.broadcasted_iota(jnp.int32, (32, 32), 1)
    want = jnp.where(dst_r < 16, 2 * dst_r, 2 * dst_r - 31)
    select = jnp.where(src_r == want, 1.0, 0.0).astype(BF16)

    def project(half):
        def ret_take(h, carry):
            own = jnp.logical_and(is_self, h == me16)

            @pl.when(own)
            def _():
                ret_local(half).wait()

            @pl.when(jnp.logical_not(own))
            def _():
                rcopy(
                    abuf.at[half, h], abuf.at[half, h],
                    ret_send.at[half, h], ret_recv.at[half, h], sib,
                ).wait_recv()

            return carry

        lax.fori_loop(0, 16, ret_take, 0)
        attn = jnp.concatenate([abuf[half, h] for h in range(HEADS)], axis=1)
        hidden = res_ref[0, 32 * half : 32 * half + 32].astype(F32) + jnp.dot(
            attn, wo_pad[...].reshape(HEADS * 128, D), preferred_element_type=F32
        )
        mean_sq = jnp.mean(hidden * hidden, axis=1, keepdims=True)
        normed = (hidden * lax.rsqrt(mean_sq + 1e-06) * gain_ref[...].reshape(1, D)).astype(BF16)
        split = jnp.dot(select, normed, preferred_element_type=F32).astype(BF16)
        for xd in range(4):
            dj, fh = xd // 2, xd % 2
            nsend[half, xd] = split[16 * dj : 16 * dj + 16, 640 * fh : 640 * fh + 640]

    def xa_copy(half, j):
        return rcopy(
            nsend.at[half, (xi + j) % 4], nall.at[xi, yi, 16 * half : 16 * half + 16],
            xa_send.at[half, j - 1], xa_recv.at[half, j - 1], xdev(j),
        )

    def xa_local(half):
        return pltpu.make_async_copy(
            nsend.at[half, xi], nall.at[xi, yi, 16 * half : 16 * half + 16], loc_sem.at[3 * half + 3]
        )

    def y_slot(half, j, dist, direction):
        xs = (xi + 4 - j) % 4
        ys = (yi - dist + 8) % 8 if direction == 0 else (yi + dist) % 8
        return nall.at[xs, ys, 16 * half : 16 * half + 16]

    def y_limit(j, direction):
        return 4 if direction == j // 2 else 3

    def y_copy(half, j, dist, direction):
        if dist == 1:
            return rcopy(
                nsend.at[half, (xi + j) % 4], nall.at[xi, yi, 16 * half : 16 * half + 16],
                y_send.at[half, j, direction, 0], y_recv.at[half, j, direction, 0],
                next_y(j, direction),
            )
        place = y_slot(half, j, dist - 1, direction)
        return rcopy(
            place, place, y_send.at[half, j, direction, dist - 1],
            y_recv.at[half, j, direction, dist - 1], y_right if direction == 0 else y_left,
        )

    def y_wait(half, j, dist, direction):
        place = y_slot(half, j, dist, direction)
        rcopy(
            place, place, y_send.at[half, j, direction, dist - 1],
            y_recv.at[half, j, direction, dist - 1], sib,
        ).wait_recv()

    for half in (0, 1):
        project(half)
        for j in (0, 1, 3, 2):
            for direction in (0, 1):
                y_copy(half, j, 1, direction).start()
        for j in (1, 3, 2):
            xa_copy(half, j).start()
        xa_local(half).start()

    for dist in (1, 2, 3, 4):
        for half in (0, 1):
            for j in (0, 1, 3, 2):
                for direction in (0, 1):
                    if dist > y_limit(j, direction):
                        continue
                    y_wait(half, j, dist, direction)
                    if dist < y_limit(j, direction):
                        y_copy(half, j, dist + 1, direction).start()
    for half in (0, 1):
        xa_local(half).wait()
        for j in (1, 2, 3):
            place = y_slot(half, j, 0, 0)
            rcopy(
                place, place, xa_send.at[half, j - 1], xa_recv.at[half, j - 1], sib
            ).wait_recv()
    for j in (1, 3, 2):
        for di in (0, 1):
            xs = (xi + 4 - j) % 4
            lines = pl.ds(pl.multiple_of((1 - core) * 80, 16), 80)
            place = wsl.at[xs, di, lines, :]
            rcopy(place, place, wf_send.at[j - 1, di], wf_recv.at[j - 1, di], sib).wait_recv()
    for di in (0, 1):
        w_local[di].wait()

    half_c = cols_n // 2
    half_f = half_c.astype(F32)

    def rs_copy(b, j):
        return rcopy(
            part_send.at[b, (xi + j) % 4], part_recv.at[b, j - 1],
            rs_send.at[b, j - 1], rs_recv.at[b, j - 1], xdev(j),
        )

    for b in range(4):
        first = (0, 128, 384, 512)[b]
        group = (128 * b + lax.broadcasted_iota(jnp.int32, (128, 512), 0)).astype(F32)
        place = (first + lax.broadcasted_iota(jnp.int32, (128, 512), 1)).astype(F32)
        band = jnp.floor((group + 0.5) / half_f)
        total = None
        window = nall[...].reshape(1024, 640)[first : first + 512]
        for di in (0, 1):
            want = band * half_f + group + di * half_f
            pick = jnp.where(place == want, 1.0, 0.0).astype(BF16)
            rows_g = jnp.dot(pick, window, preferred_element_type=F32).astype(BF16)
            term = nt(wsl[:, di].reshape(640, 640), rows_g)
            total = term if total is None else total + term
        pieces = total.reshape(4, 160, 128)
        own_part[b] = pieces
        part_send[b] = pieces.astype(BF16)
        for j in (1, 3, 2):
            rs_copy(b, j).start()

    eye = lax.broadcasted_iota(jnp.int32, (160, 160), 0) == lax.broadcasted_iota(
        jnp.int32, (160, 160), 1
    )
    pulls[4].wait()
    bias = jnp.sum(jnp.where(eye, bias_ref[...].reshape(1, 160), 0.0), axis=1, keepdims=True)
    live_groups = (rows_n // 2) * half_c
    for b in range(4):
        total = own_part[b, xi] + bias
        for j in (1, 3, 2):
            rcopy(
                part_send.at[b, 0], part_recv.at[b, j - 1],
                rs_send.at[b, j - 1], rs_recv.at[b, j - 1], sib,
            ).wait_recv()
            total = total + part_recv[b, j - 1].astype(F32)
        act = 0.5 * total * (1.0 + lax.erf(total * math.sqrt(0.5)))
        group = 128 * b + lax.broadcasted_iota(jnp.int32, (160, 128), 1)
        act = jnp.where(group < live_groups, act, 0.0)
        out_ref[0, :, 128 * b : 128 * b + 128] = act.astype(BF16)

    for n in range(15):
        p1_copy(n).wait_send()

    @pl.when(jnp.logical_not(is_self))
    def _():
        p1_copy(15).wait_send()

    def sent(s, carry):
        fw_copy(s).wait_send()
        return carry

    lax.fori_loop(0, 16, sent, 0)
    for half in (0, 1):
        for n in range(15):
            ret_copy(half, n).wait_send()

        @pl.when(jnp.logical_not(is_self))
        def _():
            ret_copy(half, 15).wait_send()

    sib_wo.wait_send()
    for dz in ZORDER:
        z_copy(dz).wait_send()
        zx_copy(dz).wait_send()
        zf_copy(dz, core).wait_send()
    for half in (0, 1):
        for j in range(4):
            for direction in (0, 1):
                for dist in range(1, y_limit(j, direction) + 1):
                    y_copy(half, j, dist, direction).wait_send()
    for j in (1, 2, 3):
        for di in (0, 1):
            xa_copy(di, j).wait_send()
            w_copy(j, di).wait_send()
            w_fwd(j, di).wait_send()
            rs_copy(di, j).wait_send()
            rs_copy(di + 2, j).wait_send()


def local(qkv_rows, residual, out_weight, norm_gain, merge_weight, merge_bias, page_grid):
    vmem = pl.BlockSpec(memory_space=pltpu.VMEM)
    dma = pltpu.SemaphoreType.DMA
    return pl.pallas_call(
        kernel,
        out_shape=jax.ShapeDtypeStruct((1, 160, 512), BF16),
        in_specs=[pl.BlockSpec(memory_space=pltpu.HBM)] * 7,
        out_specs=vmem,
        scratch_shapes=[
            pltpu.SMEM((1, 2), jnp.int32),
            pltpu.VMEM((1, 64, 3 * D), BF16),
            pltpu.VMEM((1, 64, D), BF16),
            pltpu.VMEM((D,), F32),
            pltpu.VMEM((160,), F32),
            pltpu.VMEM((16, 64, 256), BF16),
            pltpu.VMEM((2, 16, 64, 256), BF16),
            pltpu.VMEM((4, 256, 256), BF16),
            pltpu.VMEM((4, 256, 1024), F32),
            pltpu.VMEM((2, 16, 32, 128), BF16),
            pltpu.VMEM((2, 16, 32, 128), BF16),
            pltpu.VMEM((16, 128, D), BF16),
            pltpu.VMEM((4, 2, 160, 640), BF16),
            pltpu.VMEM((2, 4, 16, 640), BF16),
            pltpu.VMEM((4, 8, 32, 640), BF16),
            pltpu.VMEM((4, 4, 160, 128), F32),
            pltpu.VMEM((4, 4, 160, 128), BF16),
            pltpu.VMEM((4, 3, 160, 128), BF16),
            dma((16,)), dma((16,)), dma((16,)), dma((16,)), dma((2, 16)), dma((2, 16)),
            dma((3, 2)), dma((3, 2)), dma((3, 2)), dma((3, 2)),
            dma((7,)), dma((7,)), dma((7,)), dma((7,)), dma((7,)), dma((7,)),
            dma((2, 3)), dma((2, 3)), dma((2, 4, 2, 4)), dma((2, 4, 2, 4)), dma((4, 3)), dma((4, 3)),
            dma((12,)),
        ],
        compiler_params=pltpu.CompilerParams(
            collective_id=0, has_side_effects=True, vmem_limit_bytes=60 * 1024 * 1024
        ),
        cost_estimate=pl.CostEstimate(
            flops=4 * 10**9, bytes_accessed=4 * 10**6, transcendentals=2 * 10**6
        ),
        name="sublayer",
    )(
        page_grid, qkv_rows, residual, out_weight, norm_gain, merge_bias, merge_weight,
    )


def solution(mesh):
    in_specs = (
        P("page", "row", None),
        P("page", "row", None),
        P("page", None),
        P(),
        P("row", None),
        P("row"),
        P("page", None),
    )
    out_specs = P("page", "row", None)
    return jax.shard_map(local, mesh=mesh, in_specs=in_specs, out_specs=out_specs, check_vma=False)
```

```python
import functools
import math

import jax
import jax.numpy as jnp
from jax import lax
from jax.experimental import pallas as pl
from jax.experimental.pallas import tpu as pltpu
from jax.sharding import PartitionSpec as P

D = 1280
HEADS = 16
HDIM = 80
MESH = pl.DeviceIdType.MESH
F32 = jnp.float32
BF16 = jnp.bfloat16
BIG = -1e30
ZORDER = (1, 7, 2, 6, 3, 5, 4)
ORDER = tuple((n // 4, n % 4) for n in range(1, 16)) + ((0, 0),)


def rcopy(src, dst, send_sem, recv_sem, dev):
    return pltpu.make_async_remote_copy(
        src_ref=src, dst_ref=dst, send_sem=send_sem, recv_sem=recv_sem,
        device_id=dev, device_id_type=MESH,
    )


def nt(a, b):
    return lax.dot_general(a, b, (((1,), (1,)), ((), ())), preferred_element_type=F32)


def kernel(
    grid_hbm, qkv_hbm, res_hbm, wo_ref, gain_hbm, bias_hbm, w_ref,
    out_ref,
    grid_ref, qkv_ref, res_ref, gain_ref, bias_ref,
    pack_buf, xbuf, qbuf, sbuf, obuf, abuf, wo_pad, wsl, nsend, nall, own_part, part_send, part_recv,
    p1_send, p1_recv, fw_send, fw_recv, ret_send, ret_recv,
    w_send, w_recv, wf_send, wf_recv,
    z_send, z_recv, zx_send, zx_recv, zf_send, zf_recv,
    xa_send, xa_recv, y_send, y_recv, rs_send, rs_recv, loc_sem,
):
    page = lax.axis_index("page")
    row = lax.axis_index("row")
    core = page % 2
    zi = page // 2
    par = row % 2
    me16 = row // 2
    xi = row // 8
    yi = row % 8
    peer_page = page - core + par
    sib = (page - core + 1 - core, row)
    is_self = par == core
    y_right = (page, xi * 8 + (yi + 1) % 8)
    y_left = (page, xi * 8 + (yi + 7) % 8)

    def zdev(dz):
        return ((zi + dz) % 8 * 2 + core, row)

    def xdev(j):
        return (page, ((xi + j) % 4) * 8 + yi)

    def peer(s):
        return (peer_page, 2 * s + core)

    pulls = [
        pltpu.make_async_copy(src, dst, loc_sem.at[7 + n])
        for n, (src, dst) in enumerate(
            (
                (grid_hbm, grid_ref), (qkv_hbm, qkv_ref), (res_hbm, res_ref),
                (gain_hbm, gain_ref), (bias_hbm, bias_ref),
            )
        )
    ]
    for pull in pulls:
        pull.start()

    own_wo = pltpu.make_async_copy(wo_ref, wo_pad.at[page, 32:112, :], loc_sem.at[0])
    own_wo.start()

    barrier = pltpu.get_barrier_semaphore()

    def greet(dev):
        pl.semaphore_signal(barrier, inc=1, device_id=dev, device_id_type=MESH)

    def next_y(j, direction):
        return (page, (xi + j) % 4 * 8 + (yi + 1 + 6 * direction) % 8)

    greet(sib)
    for dz in ZORDER:
        greet(zdev(dz))
    for j in range(4):
        greet(next_y(j, 0))
        greet(next_y(j, 1))

    def greet_peer(i, carry):
        greet(peer((me16 + i) % 16))
        return carry

    lax.fori_loop(1, 16, greet_peer, 0)

    @pl.when(jnp.logical_not(is_self))
    def _():
        greet(peer(me16))
        for j in (1, 2, 3):
            greet(xdev(j))

    pulls[0].wait()
    rows_n = grid_ref[0, 0]
    cols_n = grid_ref[0, 1]
    valid_len = rows_n * cols_n
    lane = lax.broadcasted_iota(jnp.int32, (64, 256), 1)
    slot = row * 64 + lax.broadcasted_iota(jnp.int32, (64, 256), 0)
    tail = jnp.where(
        lane == 240, jnp.where(slot < valid_len, 0.0, BIG), jnp.where(lane == 241, 1.0, 0.0)
    )

    def pack(h):
        val = tail
        for third in (2, 1, 0):
            start = third * D + h * HDIM
            base = pl.multiple_of(jnp.minimum(start // 128 * 128, 3 * D - 256), 128)
            dest = third * HDIM
            window = qkv_ref[0, :, pl.ds(base, 256)].astype(F32)
            window = pltpu.roll(window, (dest + 256 - (start - base)) % 256, axis=1)
            val = jnp.where((lane >= dest) & (lane < dest + HDIM), window, val)
        pack_buf[h] = val.astype(BF16)

    @pl.when(is_self)
    def _():
        pl.semaphore_wait(barrier, 31)

    @pl.when(jnp.logical_not(is_self))
    def _():
        pl.semaphore_wait(barrier, 35)

    my_col = pl.multiple_of(xi % 2 * 640, 128)
    other_col = pl.multiple_of(640 - xi % 2 * 640, 128)
    x_side = (page, (xi + 5 - 2 * core) % 4 * 8 + yi)

    def z_page(dz, of_core):
        return (zi + 8 - dz) % 8 * 2 + of_core

    def z_copy(dz):
        return rcopy(
            wo_pad.at[page, 32:112, pl.ds(my_col, 640)], wo_pad.at[page, 32:112, pl.ds(my_col, 640)],
            z_send.at[dz - 1], z_recv.at[dz - 1], zdev(dz),
        )

    def zx_copy(dz):
        place = wo_pad.at[z_page(dz, core), 32:112, pl.ds(my_col, 640)]
        return rcopy(place, place, zx_send.at[dz - 1], zx_recv.at[dz - 1], x_side)

    def zf_copy(dz, of_core):
        place = wo_pad.at[z_page(dz, of_core), 32:112, :]
        return rcopy(place, place, zf_send.at[dz - 1], zf_recv.at[dz - 1], sib)

    def z_step(dz):
        place = wo_pad.at[z_page(dz, core), 32:112, pl.ds(my_col, 640)]
        rcopy(place, place, z_send.at[dz - 1], z_recv.at[dz - 1], sib).wait_recv()
        zx_copy(dz).start()

    def zx_step(dz):
        place = wo_pad.at[z_page(dz, core), 32:112, pl.ds(other_col, 640)]
        rcopy(place, place, zx_send.at[dz - 1], zx_recv.at[dz - 1], sib).wait_recv()
        zf_copy(dz, core).start()

    half_y = yi // 2

    def p1_copy(n):
        dx, dy = ORDER[n]
        h = (xi + dx) % 4 * 4 + (half_y + dy) % 4
        return rcopy(
            pack_buf.at[h], xbuf.at[0, me16], p1_send.at[h], p1_recv.at[me16], peer(h)
        )

    p1_local = pltpu.make_async_copy(pack_buf.at[me16], xbuf.at[0, me16], p1_recv.at[me16])

    own_wo.wait()
    for dz in ZORDER:
        z_copy(dz).start()
    pulls[1].wait()
    for n in range(15):
        dx, dy = ORDER[n]
        pack((xi + dx) % 4 * 4 + (half_y + dy) % 4)
        p1_copy(n).start()
    pack(me16)

    @pl.when(is_self)
    def _():
        p1_local.start()

    @pl.when(jnp.logical_not(is_self))
    def _():
        p1_copy(15).start()


    def w_copy(j, di):
        xd = (xi + j) % 4
        col = pl.multiple_of((2 * di + xd // 2) * D + (xd % 2) * 640, 128)
        lines = pl.ds(pl.multiple_of(core * 80, 16), 80)
        return rcopy(
            w_ref.at[lines, pl.ds(col, 640)], wsl.at[xi, di, lines, :],
            w_send.at[j - 1, di], w_recv.at[j - 1, di], xdev(j),
        )

    def w_fwd(j, di):
        xs = (xi + 4 - j) % 4
        lines = pl.ds(pl.multiple_of(core * 80, 16), 80)
        place = wsl.at[xs, di, lines, :]
        return rcopy(place, place, wf_send.at[j - 1, di], wf_recv.at[j - 1, di], sib)

    for j in (1, 3, 2):
        for di in (0, 1):
            w_copy(j, di).start()
    w_local = []
    for di in (0, 1):
        col = pl.multiple_of((2 * di + xi // 2) * D + (xi % 2) * 640, 128)
        w_local.append(
            pltpu.make_async_copy(w_ref.at[:, pl.ds(col, 640)], wsl.at[xi, di], loc_sem.at[4 + di])
        )
        w_local[di].start()
    sib_wo = rcopy(wo_pad.at[page, 32:112, :], wo_pad.at[page, 32:112, :], loc_sem.at[1], loc_sem.at[2], sib)
    sib_wo.start()
    for h in range(HEADS):
        wo_pad[h, 0:32, :] = jnp.zeros((32, D), BF16)
        wo_pad[h, 112:128, :] = jnp.zeros((16, D), BF16)

    def fw_copy(s):
        return rcopy(xbuf.at[0, s], xbuf.at[1, s], fw_send.at[s], fw_recv.at[s], sib)

    def p1_take(n):
        dx, dy = ORDER[n]
        s = (xi + 4 - dx) % 4 * 4 + (half_y + 4 - dy) % 4
        rcopy(xbuf.at[0, s], xbuf.at[0, s], p1_send.at[s], p1_recv.at[s], sib).wait_recv()
        fw_copy(s).start()

    @pl.when(is_self)
    def _():
        p1_local.wait()
        fw_copy(me16).start()

    for n in range(15):
        p1_take(n)

    @pl.when(jnp.logical_not(is_self))
    def _():
        p1_take(15)

    for dz in ZORDER:
        z_step(dz)

    factor = math.log2(math.e) / math.sqrt(HDIM)
    lane_q = lax.broadcasted_iota(jnp.int32, (256, 256), 1)

    def owner(n):
        dx, dy = ORDER[n]
        return (xi + dx) % 4 * 4 + (half_y + dy) % 4

    def ret_copy(half, n):
        return rcopy(
            obuf.at[half, n], abuf.at[half, me16],
            ret_send.at[half, n], ret_recv.at[half, me16], peer(owner(n)),
        )

    def ret_local(half):
        return pltpu.make_async_copy(
            obuf.at[half, 15], abuf.at[half, me16], ret_recv.at[half, me16]
        )

    def rolled_queries(blk):
        half, first = blk // 2, blk % 2 * 8
        queries = jnp.concatenate(
            [xbuf[0, owner(n), 32 * half : 32 * half + 32] for n in range(first, first + 8)], axis=0
        )
        rolled = pltpu.roll(queries.astype(F32), HDIM, axis=1)
        return jnp.where(
            (lane_q >= HDIM) & (lane_q < 2 * HDIM), rolled, jnp.where(lane_q == 240, 1.0, 0.0)
        ).astype(BF16)

    for blk in range(4):
        qbuf[blk] = rolled_queries(blk)
        sbuf[blk] = nt(qbuf[blk], xbuf[0].reshape(1024, 256))

    def fw_take(s, carry):
        rcopy(xbuf.at[1, s], xbuf.at[1, s], fw_send.at[s], fw_recv.at[s], sib).wait_recv()
        return carry

    lax.fori_loop(0, 16, fw_take, 0)
    later = nt(qbuf[0], xbuf[1].reshape(1024, 256))
    for blk in range(4):
        there = later
        if blk < 3:
            later = nt(qbuf[blk + 1], xbuf[1].reshape(1024, 256))
        here = sbuf[blk]
        peak = jnp.maximum(
            jnp.max(here, axis=1, keepdims=True), jnp.max(there, axis=1, keepdims=True)
        )
        mixed = jnp.dot(
            jnp.exp2((here - peak) * factor).astype(BF16), xbuf[0].reshape(1024, 256),
            preferred_element_type=F32,
        ) + jnp.dot(
            jnp.exp2((there - peak) * factor).astype(BF16), xbuf[1].reshape(1024, 256),
            preferred_element_type=F32,
        )
        mixed = mixed[:, 128:]
        mixed = mixed / mixed[:, 113:114]
        half, first = blk // 2, blk % 2 * 8
        obuf[half, first : first + 8] = mixed.astype(BF16).reshape(8, 32, 128)
        for n in range(first, min(first + 8, 15)):
            ret_copy(half, n).start()

    @pl.when(is_self)
    def _():
        ret_local(0).start()
        ret_local(1).start()

    @pl.when(jnp.logical_not(is_self))
    def _():
        ret_copy(0, 15).start()
        ret_copy(1, 15).start()

    for dz in ZORDER:
        zx_step(dz)

    for j in (1, 3, 2):
        for di in (0, 1):
            xs = (xi + 4 - j) % 4
            lines = pl.ds(pl.multiple_of(core * 80, 16), 80)
            place = wsl.at[xs, di, lines, :]
            rcopy(place, place, w_send.at[j - 1, di], w_recv.at[j - 1, di], sib).wait_recv()
            w_fwd(j, di).start()

    sib_page = page - core + 1 - core
    rcopy(wo_ref, wo_pad.at[sib_page, 32:112, :], loc_sem.at[1], loc_sem.at[2], sib).wait_recv()
    for dz in ZORDER:
        zf_copy(dz, 1 - core).wait_recv()
    pulls[2].wait()
    pulls[3].wait()
    dst_r = lax.broadcasted_iota(jnp.int32, (32, 32), 0)
    src_r = lax.broadcasted_iota(jnp.int32, (32, 32), 1)
    want = jnp.where(dst_r < 16, 2 * dst_r, 2 * dst_r - 31)
    select = jnp.where(src_r == want, 1.0, 0.0).astype(BF16)

    def project(half):
        def ret_take(h, carry):
            own = jnp.logical_and(is_self, h == me16)

            @pl.when(own)
            def _():
                ret_local(half).wait()

            @pl.when(jnp.logical_not(own))
            def _():
                rcopy(
                    abuf.at[half, h], abuf.at[half, h],
                    ret_send.at[half, h], ret_recv.at[half, h], sib,
                ).wait_recv()

            return carry

        lax.fori_loop(0, 16, ret_take, 0)
        attn = jnp.concatenate([abuf[half, h] for h in range(HEADS)], axis=1)
        hidden = res_ref[0, 32 * half : 32 * half + 32].astype(F32) + jnp.dot(
            attn, wo_pad[...].reshape(HEADS * 128, D), preferred_element_type=F32
        )
        mean_sq = jnp.mean(hidden * hidden, axis=1, keepdims=True)
        normed = (hidden * lax.rsqrt(mean_sq + 1e-06) * gain_ref[...].reshape(1, D)).astype(BF16)
        split = jnp.dot(select, normed, preferred_element_type=F32).astype(BF16)
        for xd in range(4):
            dj, fh = xd // 2, xd % 2
            nsend[half, xd] = split[16 * dj : 16 * dj + 16, 640 * fh : 640 * fh + 640]

    def xa_copy(half, j):
        return rcopy(
            nsend.at[half, (xi + j) % 4], nall.at[xi, yi, 16 * half : 16 * half + 16],
            xa_send.at[half, j - 1], xa_recv.at[half, j - 1], xdev(j),
        )

    def xa_local(half):
        return pltpu.make_async_copy(
            nsend.at[half, xi], nall.at[xi, yi, 16 * half : 16 * half + 16], loc_sem.at[3 * half + 3]
        )

    def y_slot(half, j, dist, direction):
        xs = (xi + 4 - j) % 4
        ys = (yi - dist + 8) % 8 if direction == 0 else (yi + dist) % 8
        return nall.at[xs, ys, 16 * half : 16 * half + 16]

    def y_limit(j, direction):
        return 4 if direction == j // 2 else 3

    def y_copy(half, j, dist, direction):
        if dist == 1:
            return rcopy(
                nsend.at[half, (xi + j) % 4], nall.at[xi, yi, 16 * half : 16 * half + 16],
                y_send.at[half, j, direction, 0], y_recv.at[half, j, direction, 0],
                next_y(j, direction),
            )
        place = y_slot(half, j, dist - 1, direction)
        return rcopy(
            place, place, y_send.at[half, j, direction, dist - 1],
            y_recv.at[half, j, direction, dist - 1], y_right if direction == 0 else y_left,
        )

    def y_wait(half, j, dist, direction):
        place = y_slot(half, j, dist, direction)
        rcopy(
            place, place, y_send.at[half, j, direction, dist - 1],
            y_recv.at[half, j, direction, dist - 1], sib,
        ).wait_recv()

    for half in (0, 1):
        project(half)
        for j in (0, 1, 3, 2):
            for direction in (0, 1):
                y_copy(half, j, 1, direction).start()
        for j in (1, 3, 2):
            xa_copy(half, j).start()
        xa_local(half).start()

    for dist in (1, 2, 3, 4):
        for half in (0, 1):
            for j in (0, 1, 3, 2):
                for direction in (0, 1):
                    if dist > y_limit(j, direction):
                        continue
                    y_wait(half, j, dist, direction)
                    if dist < y_limit(j, direction):
                        y_copy(half, j, dist + 1, direction).start()
    for half in (0, 1):
        xa_local(half).wait()
        for j in (1, 2, 3):
            place = y_slot(half, j, 0, 0)
            rcopy(
                place, place, xa_send.at[half, j - 1], xa_recv.at[half, j - 1], sib
            ).wait_recv()
    for j in (1, 3, 2):
        for di in (0, 1):
            xs = (xi + 4 - j) % 4
            lines = pl.ds(pl.multiple_of((1 - core) * 80, 16), 80)
            place = wsl.at[xs, di, lines, :]
            rcopy(place, place, wf_send.at[j - 1, di], wf_recv.at[j - 1, di], sib).wait_recv()
    for di in (0, 1):
        w_local[di].wait()

    half_c = cols_n // 2
    half_f = half_c.astype(F32)

    def rs_copy(b, j):
        return rcopy(
            part_send.at[b, (xi + j) % 4], part_recv.at[b, j - 1],
            rs_send.at[b, j - 1], rs_recv.at[b, j - 1], xdev(j),
        )

    for b in range(4):
        first = (0, 128, 384, 512)[b]
        group = (128 * b + lax.broadcasted_iota(jnp.int32, (128, 512), 0)).astype(F32)
        place = (first + lax.broadcasted_iota(jnp.int32, (128, 512), 1)).astype(F32)
        band = jnp.floor((group + 0.5) / half_f)
        total = None
        window = nall[...].reshape(1024, 640)[first : first + 512]
        for di in (0, 1):
            want = band * half_f + group + di * half_f
            pick = jnp.where(place == want, 1.0, 0.0).astype(BF16)
            rows_g = jnp.dot(pick, window, preferred_element_type=F32).astype(BF16)
            term = nt(wsl[:, di].reshape(640, 640), rows_g)
            total = term if total is None else total + term
        pieces = total.reshape(4, 160, 128)
        own_part[b] = pieces
        part_send[b] = pieces.astype(BF16)
        for j in (1, 3, 2):
            rs_copy(b, j).start()

    for n in range(15):
        p1_copy(n).wait_send()

    @pl.when(jnp.logical_not(is_self))
    def _():
        p1_copy(15).wait_send()

    def sent(s, carry):
        fw_copy(s).wait_send()
        return carry

    lax.fori_loop(0, 16, sent, 0)
    for half in (0, 1):
        for n in range(15):
            ret_copy(half, n).wait_send()

        @pl.when(jnp.logical_not(is_self))
        def _():
            ret_copy(half, 15).wait_send()

    sib_wo.wait_send()
    for dz in ZORDER:
        z_copy(dz).wait_send()
        zx_copy(dz).wait_send()
        zf_copy(dz, core).wait_send()
    for half in (0, 1):
        for j in range(4):
            for direction in (0, 1):
                for dist in range(1, y_limit(j, direction) + 1):
                    y_copy(half, j, dist, direction).wait_send()
    for j in (1, 2, 3):
        for di in (0, 1):
            xa_copy(di, j).wait_send()
            w_copy(j, di).wait_send()
            w_fwd(j, di).wait_send()

    eye = lax.broadcasted_iota(jnp.int32, (160, 160), 0) == lax.broadcasted_iota(
        jnp.int32, (160, 160), 1
    )
    pulls[4].wait()
    bias = jnp.sum(jnp.where(eye, bias_ref[...].reshape(1, 160), 0.0), axis=1, keepdims=True)
    live_groups = (rows_n // 2) * half_c
    for b in range(4):
        total = own_part[b, xi] + bias
        for j in (1, 3, 2):
            rcopy(
                part_send.at[b, 0], part_recv.at[b, j - 1],
                rs_send.at[b, j - 1], rs_recv.at[b, j - 1], sib,
            ).wait_recv()
            total = total + part_recv[b, j - 1].astype(F32)
        act = 0.5 * total * (1.0 + lax.erf(total * math.sqrt(0.5)))
        group = 128 * b + lax.broadcasted_iota(jnp.int32, (160, 128), 1)
        act = jnp.where(group < live_groups, act, 0.0)
        out_ref[0, :, 128 * b : 128 * b + 128] = act.astype(BF16)

    for b in range(4):
        for j in (1, 2, 3):
            rs_copy(b, j).wait_send()


def local(qkv_rows, residual, out_weight, norm_gain, merge_weight, merge_bias, page_grid):
    vmem = pl.BlockSpec(memory_space=pltpu.VMEM)
    dma = pltpu.SemaphoreType.DMA
    return pl.pallas_call(
        kernel,
        out_shape=jax.ShapeDtypeStruct((1, 160, 512), BF16),
        in_specs=[pl.BlockSpec(memory_space=pltpu.HBM)] * 7,
        out_specs=vmem,
        scratch_shapes=[
            pltpu.SMEM((1, 2), jnp.int32),
            pltpu.VMEM((1, 64, 3 * D), BF16),
            pltpu.VMEM((1, 64, D), BF16),
            pltpu.VMEM((D,), F32),
            pltpu.VMEM((160,), F32),
            pltpu.VMEM((16, 64, 256), BF16),
            pltpu.VMEM((2, 16, 64, 256), BF16),
            pltpu.VMEM((4, 256, 256), BF16),
            pltpu.VMEM((4, 256, 1024), F32),
            pltpu.VMEM((2, 16, 32, 128), BF16),
            pltpu.VMEM((2, 16, 32, 128), BF16),
            pltpu.VMEM((16, 128, D), BF16),
            pltpu.VMEM((4, 2, 160, 640), BF16),
            pltpu.VMEM((2, 4, 16, 640), BF16),
            pltpu.VMEM((4, 8, 32, 640), BF16),
            pltpu.VMEM((4, 4, 160, 128), F32),
            pltpu.VMEM((4, 4, 160, 128), BF16),
            pltpu.VMEM((4, 3, 160, 128), BF16),
            dma((16,)), dma((16,)), dma((16,)), dma((16,)), dma((2, 16)), dma((2, 16)),
            dma((3, 2)), dma((3, 2)), dma((3, 2)), dma((3, 2)),
            dma((7,)), dma((7,)), dma((7,)), dma((7,)), dma((7,)), dma((7,)),
            dma((2, 3)), dma((2, 3)), dma((2, 4, 2, 4)), dma((2, 4, 2, 4)), dma((4, 3)), dma((4, 3)),
            dma((12,)),
        ],
        compiler_params=pltpu.CompilerParams(
            collective_id=0, has_side_effects=True, vmem_limit_bytes=60 * 1024 * 1024
        ),
        cost_estimate=pl.CostEstimate(
            flops=4 * 10**9, bytes_accessed=4 * 10**6, transcendentals=2 * 10**6
        ),
        name="sublayer",
    )(
        page_grid, qkv_rows, residual, out_weight, norm_gain, merge_bias, merge_weight,
    )


def solution(mesh):
    in_specs = (
        P("page", "row", None),
        P("page", "row", None),
        P("page", None),
        P(),
        P("row", None),
        P("row"),
        P("page", None),
    )
    out_specs = P("page", "row", None)
    return jax.shard_map(local, mesh=mesh, in_specs=in_specs, out_specs=out_specs, check_vma=False)
```
